256 devices in a mesh: grp: 32 (over x, y, core), sp: 8 (over z).
Axes of the slice: x: 4, y: 4, z: 8, core: 2. Of those that a mesh axis runs over, the one named last changes fastest.
Arguments:
- queries: bfloat16 [32768, 2048], P(('grp', 'sp')), may hold values from -170 to 170
- key_rows: bfloat16 [32768, 2048], P(('grp', 'sp')), may hold values from -7 to 7
- value_rows: bfloat16 [32768, 2048], P(('grp', 'sp')), may hold values from -6 to 6
- upstream: bfloat16 [32768, 2048], P(('grp', 'sp')), may hold values from -6 to 6
- neighbours: int32 [256, 8], P('grp'), may hold values from 0 to 255, as said below
- counts: int32 [256], P('grp'), may hold values from 1 to 8, as said below
Outputs:
- attended: bfloat16 [32768, 2048], P(('grp', 'sp'))
- query_grad: bfloat16 [32768, 2048], P(('grp', 'sp'))
- key_grad: bfloat16 [32768, 2048], P(('grp', 'sp'))
- value_grad: bfloat16 [32768, 2048], P(('grp', 'sp'))
The draws below stay inside these ranges and needn't reach their ends.
Inputs may be any that keep to these rules, and one draw needn't show every extreme that they name: `neighbours`: row b names block b in slot 0 and then distinct blocks of b's group of 8 blocks or of the two groups beside it; slots past counts[b] hold such blocks too and are not used. `counts`: every group of 8 blocks has a block with all 8 slots used.
All inputs are finite; a program needn't handle non-finite values.
Results may differ from the reference program's by a relative error of at most 0.034.
Values may be sent and summed in bfloat16 or wider, within the bound.
No kernel may reach another device: no remote copies, remote signals or barrier semaphores. Data moves between devices by JAX's collectives and lax.ppermute only.
A program may use at most 128 MiB of HBM per device.

```python
import jax
import jax.numpy as jnp
from jax import lax

H = 16
HD = 128
D = 2048
BLK = 128
NNB = 8
NB_G = 8
NBLK = 256
TOKENS = 32768
N_GRP = 32


def shared_keys(key):
    return jnp.clip(jax.random.normal(key, (TOKENS, D), jnp.float32), -6.0, 6.0)


def draw_key_rows(key, part):
    base = shared_keys(key)
    return base.astype(jnp.bfloat16)


def draw_queries(key, part):
    key = jax.random.fold_in(key, 7)
    drawn = jnp.clip(jax.random.normal(key, (TOKENS, D), jnp.float32), -6.0, 6.0)
    return drawn.astype(jnp.bfloat16)


def draw_neighbours(key, part):
    key = jax.random.fold_in(key, 3)
    blocks = jnp.arange(NBLK, dtype=jnp.int32)
    group_start = blocks // NB_G * NB_G
    lowest = jnp.maximum(group_start - NB_G, 0)
    highest = jnp.minimum(group_start + 2 * NB_G, NBLK)
    offsets = jnp.arange(3 * NB_G, dtype=jnp.int32)
    candidate = lowest[:, None] + offsets[None, :]
    allowed = (candidate < highest[:, None]) & (candidate != blocks[:, None])
    noise = jax.random.randint(key, (NBLK, 3 * NB_G), 0, 1 << 20, dtype=jnp.int32)
    ranking = jnp.where(allowed, noise * (3 * NB_G) + offsets[None, :], -1 - offsets[None, :])
    chosen = lax.top_k(ranking, NNB - 1)[1].astype(jnp.int32)
    picked = jnp.take_along_axis(candidate, chosen, axis=1)
    return jnp.concatenate([blocks[:, None], picked], axis=1).astype(jnp.int32)


def draw_counts(key, part):
    key = jax.random.fold_in(key, 5)
    blocks = jnp.arange(NBLK, dtype=jnp.int32)
    drawn = jax.random.randint(key, (NBLK,), 1, NNB + 1, dtype=jnp.int32)
    return jnp.where(blocks % NB_G == 0, NNB, drawn).astype(jnp.int32)


def steps_of(stream_key, extent, shards, smallest, high):
    def one(axis_at, blocks):
        heights = jax.random.uniform(jax.random.fold_in(jax.random.fold_in(stream_key, 6), axis_at), (blocks,), jnp.float32, smallest / len(shards), high / len(shards))
        return jnp.repeat(jnp.exp(heights), extent[axis_at] // blocks).reshape((-1,) + (1,) * (len(extent) - axis_at - 1))

    level = one(*shards[0])
    for cut in shards[1:]:
        level = level * one(*cut)
    return level


def gaussian(rng, extent, deviation, limit, split=(), held_as=jnp.bfloat16):
    values = deviation * jax.random.normal(rng, extent, jnp.float32)
    if split:
        values = values * steps_of(rng, extent, split, -0.22, 0.18)
    return jnp.clip(values, -limit, limit).astype(held_as)


def setup_inputs(seed: int = 0) -> dict:
    streams_of = jax.random.split(jax.random.key(seed), 7)
    return {
        "queries": draw_queries(jax.random.fold_in(streams_of[6], 71), 0),
        "key_rows": draw_key_rows(jax.random.fold_in(streams_of[6], 71), 0),
        "value_rows": gaussian(streams_of[2], (TOKENS, D), 1.0, 6.0, ((0, 256),)),
        "upstream": gaussian(streams_of[3], (TOKENS, D), 1.0, 6.0, ((0, 256),)),
        "neighbours": draw_neighbours(jax.random.fold_in(streams_of[6], 71), 0),
        "counts": draw_counts(jax.random.fold_in(streams_of[6], 71), 0),
    }


def block_probability(query_tile, key_tiles, usable):
    scores = jnp.einsum("qhd,khd->hqk", query_tile, key_tiles) * (HD ** -0.5)
    allowed = jnp.repeat(usable, BLK)
    scores = jnp.where(allowed[None, None, :], scores, -1e30)
    highest = jnp.max(scores, axis=-1, keepdims=True)
    raised = jnp.exp(scores - highest)
    return raised / jnp.sum(raised, axis=-1, keepdims=True)


def rounded(table):
    return lax.optimization_barrier(table.astype(jnp.bfloat16)).astype(jnp.float32)


def reference(queries, key_rows, value_rows, upstream, neighbours, counts):
    scaling = HD ** -0.5
    query_blocks = queries.reshape(NBLK, BLK, H, HD)
    key_blocks = key_rows.reshape(NBLK, BLK, H, HD)
    value_blocks = value_rows.reshape(NBLK, BLK, H, HD)
    grad_blocks = upstream.reshape(NBLK, BLK, H, HD)
    usable_all = jnp.arange(NNB)[None, :] < counts[:, None]

    def pick_rows(table, slot_ids):
        return table[slot_ids].reshape(NNB * BLK, H, HD).astype(jnp.float32)

    def forward_block(pieces):
        query_tile, slot_ids, usable = pieces
        key_tiles = pick_rows(key_blocks, slot_ids)
        value_tiles = pick_rows(value_blocks, slot_ids)
        probability = block_probability(query_tile.astype(jnp.float32), key_tiles, usable)
        weights = lax.optimization_barrier(probability.astype(jnp.bfloat16)).astype(jnp.float32)
        return jnp.einsum("hqk,khd->qhd", weights, value_tiles).astype(jnp.bfloat16)

    attended = lax.map(forward_block, (query_blocks, neighbours, usable_all))
    row_delta = jnp.sum(grad_blocks.astype(jnp.float32) * attended.astype(jnp.float32), axis=-1)

    def group_step(carry, group_id):
        key_sum, value_sum = carry
        anchor = ((group_id - 1) * NB_G).astype(jnp.int32)
        first = (group_id * NB_G).astype(jnp.int32)

        def cut(array):
            return lax.dynamic_slice_in_dim(array, first, NB_G, 0)

        def backward_block(inner, pieces):
            key_loc, value_loc = inner
            query_tile, grad_tile, delta_tile, slot_ids, usable = pieces
            query_f = query_tile.astype(jnp.float32)
            grad_f = grad_tile.astype(jnp.float32)
            key_tiles = pick_rows(key_blocks, slot_ids)
            value_tiles = pick_rows(value_blocks, slot_ids)
            probability = block_probability(query_f, key_tiles, usable)
            weights = lax.optimization_barrier(probability.astype(jnp.bfloat16)).astype(jnp.float32)
            grad_prob = jnp.einsum("qhd,khd->hqk", grad_f, value_tiles)
            grad_score = probability * (grad_prob - delta_tile.T[:, :, None])
            grad_score = lax.optimization_barrier(grad_score.astype(jnp.bfloat16)).astype(jnp.float32)
            query_part = (jnp.einsum("hqk,khd->qhd", grad_score, key_tiles) * scaling).astype(jnp.bfloat16)
            key_part = jnp.einsum("hqk,qhd->khd", grad_score, query_f) * scaling
            value_part = jnp.einsum("hqk,qhd->khd", weights, grad_f)
            local_ids = (slot_ids - anchor).astype(jnp.int32)
            key_loc = key_loc.at[local_ids].add(key_part.reshape(NNB, BLK, H, HD))
            value_loc = value_loc.at[local_ids].add(value_part.reshape(NNB, BLK, H, HD))
            return (key_loc, value_loc), query_part

        local_zeros = jnp.zeros((3 * NB_G, BLK, H, HD), jnp.float32)
        (key_loc, value_loc), query_part = lax.scan(
            backward_block, (local_zeros, local_zeros),
            (cut(query_blocks), cut(grad_blocks), cut(row_delta), cut(neighbours), cut(usable_all)))

        def settle(table):
            return jnp.concatenate([rounded(table[:NB_G]), table[NB_G:2 * NB_G],
                                    rounded(table[2 * NB_G:])], axis=0)

        def place(total, local):
            window = lax.dynamic_slice_in_dim(total, first, 3 * NB_G, 0)
            return lax.dynamic_update_slice_in_dim(total, window + settle(local), first, 0)

        return (place(key_sum, key_loc), place(value_sum, value_loc)), query_part

    zeros = jnp.zeros((NBLK + 2 * NB_G, BLK, H, HD), jnp.float32)
    (key_sum, value_sum), query_grad = lax.scan(
        group_step, (zeros, zeros), jnp.arange(N_GRP, dtype=jnp.int32))
    key_sum = key_sum[NB_G:NB_G + NBLK]
    value_sum = value_sum[NB_G:NB_G + NBLK]
    return (attended.reshape(TOKENS, D), query_grad.reshape(TOKENS, D),
            key_sum.astype(jnp.bfloat16).reshape(TOKENS, D),
            value_sum.astype(jnp.bfloat16).reshape(TOKENS, D))
```

```python
import functools

import jax
import jax.numpy as jnp
from jax import lax
from jax.experimental import pallas as pl
from jax.experimental.pallas import tpu as pltpu
from jax.sharding import PartitionSpec as P

H = 16
HD = 128
BLK = 128
NNB = 8
SCALE = HD ** (-0.5)
LOG2E = 1.4426950408889634
NT = (((1,), (1,)), ((), ()))
NN = (((1,), (0,)), ((), ()))
TN = (((0,), (0,)), ((), ()))
F32 = jnp.float32
BF16 = jnp.bfloat16
ANY = pl.BlockSpec(memory_space=pl.ANY)
SMEM = pl.BlockSpec(memory_space=pltpu.SMEM)
VMEM = pl.BlockSpec(memory_space=pltpu.VMEM)
LIMIT = 48 * 1024 * 1024


def dot(a, b, dims):
    return lax.dot_general(a, b, dims, preferred_element_type=F32)


def run_copies(copies):
    for copy in copies:
        copy.start()
    for copy in copies:
        copy.wait()


def pack_kernel(phase, heads_dev, sp, *refs):
    sources, out, sems = refs[:4], refs[4], refs[5]
    copies = []
    for i, source in enumerate(sources):
        for j in range(sp):
            head = j * heads_dev + phase
            copies.append(
                pltpu.make_async_copy(
                    source.at[:, pl.ds(head * HD, HD)], out.at[j, i], sems.at[i, j]
                )
            )
    run_copies(copies)


def pack(arrays, phase, heads_dev, sp):
    rows = arrays[0].shape[0]
    return pl.pallas_call(
        functools.partial(pack_kernel, phase, heads_dev, sp),
        out_shape=jax.ShapeDtypeStruct((sp, 4, rows, HD), BF16),
        in_specs=[ANY] * 4,
        out_specs=ANY,
        scratch_shapes=[pltpu.SemaphoreType.DMA((4, sp))],
        name="pack",
    )(*arrays)


def unpack_kernel(phase, heads_dev, sp, received, *refs):
    outs, sems = refs[-5:-1], refs[-1]
    copies = []
    for i, out in enumerate(outs):
        for j in range(sp):
            head = j * heads_dev + phase
            copies.append(
                pltpu.make_async_copy(
                    received.at[j, i], out.at[:, pl.ds(head * HD, HD)], sems.at[i, j]
                )
            )
    run_copies(copies)


def unpack(received, held, phase, heads_dev, sp):
    rows = received.shape[2]
    shape = jax.ShapeDtypeStruct((rows, sp * heads_dev * HD), BF16)
    return pl.pallas_call(
        functools.partial(unpack_kernel, phase, heads_dev, sp),
        out_shape=[shape] * 4,
        in_specs=[ANY] * (1 + len(held)),
        out_specs=[ANY] * 4,
        input_output_aliases={1 + i: i for i in range(len(held))},
        scratch_shapes=[pltpu.SemaphoreType.DMA((4, sp))],
        name="unpack",
    )(received, *held)


def attn_kernel(
    nb, ids, counts, own, before, after, main, grad_own, grad_before, grad_after,
    keys, values, key_acc, value_acc, sems,
):
    copies = []
    for i, table in enumerate((keys, values)):
        for g, source in enumerate((before.at[:, i], own.at[:, i], after.at[:, i])):
            copies.append(
                pltpu.make_async_copy(source, table.at[pl.ds(g * nb, nb)], sems.at[i, g])
            )
    for copy in copies:
        copy.start()
    key_acc[...] = jnp.zeros_like(key_acc)
    value_acc[...] = jnp.zeros_like(value_acc)
    for copy in copies:
        copy.wait()

    def block(b, carry):
        count = counts[b]
        query = own[b, 2]
        grad = own[b, 3]
        slots = [ids[b, j] for j in range(NNB)]
        key_cat = jnp.concatenate([keys[s] for s in slots], axis=0)
        value_cat = jnp.concatenate([values[s] for s in slots], axis=0)
        raw = dot(query, key_cat, NT)
        slot_of = lax.broadcasted_iota(jnp.int32, (1, NNB * BLK), 1) // BLK
        raw = jnp.where(slot_of < count, raw, -1e30)
        highest = jnp.max(raw, axis=1, keepdims=True)
        raised = jnp.exp2((raw - highest) * (SCALE * LOG2E))
        total = jnp.sum(raised, axis=1, keepdims=True)
        prob = raised * (1.0 / total)
        weights = prob.astype(BF16)
        attended = dot(weights, value_cat, NN).astype(BF16)
        delta = jnp.sum(grad.astype(F32) * attended.astype(F32), axis=1, keepdims=True)
        grad_prob = dot(grad, value_cat, NT)
        score = (prob * (grad_prob - delta)).astype(BF16)
        main[b, 0] = attended
        main[b, 1] = (dot(score, key_cat, NN) * SCALE).astype(BF16)
        key_part = dot(score, query, TN)
        value_part = dot(weights, grad, TN)
        for j, s in enumerate(slots):
            key_acc[s] += key_part[j * BLK:(j + 1) * BLK]
            value_acc[s] += value_part[j * BLK:(j + 1) * BLK]
        return carry

    lax.fori_loop(0, nb, block, 0)
    for g, (out, kind) in enumerate(((grad_before, BF16), (grad_own, F32), (grad_after, BF16))):
        out[:, 0] = (key_acc[g * nb:(g + 1) * nb] * SCALE).astype(kind)
        out[:, 1] = value_acc[g * nb:(g + 1) * nb].astype(kind)


def attention(ids, counts, own, before, after):
    nb = own.shape[0]
    pair = (nb, 2, BLK, HD)
    return pl.pallas_call(
        functools.partial(attn_kernel, nb),
        out_shape=[
            jax.ShapeDtypeStruct(pair, BF16),
            jax.ShapeDtypeStruct(pair, F32),
            jax.ShapeDtypeStruct(pair, BF16),
            jax.ShapeDtypeStruct(pair, BF16),
        ],
        in_specs=[SMEM, SMEM, VMEM, ANY, ANY],
        out_specs=[VMEM] * 4,
        scratch_shapes=[
            pltpu.VMEM((3 * nb, BLK, HD), BF16),
            pltpu.VMEM((3 * nb, BLK, HD), BF16),
            pltpu.VMEM((3 * nb, BLK, HD), F32),
            pltpu.VMEM((3 * nb, BLK, HD), F32),
            pltpu.SemaphoreType.DMA((2, 3)),
        ],
        compiler_params=pltpu.CompilerParams(vmem_limit_bytes=LIMIT),
        cost_estimate=pl.CostEstimate(
            flops=12 * nb * NNB * BLK * BLK * HD,
            bytes_accessed=6 * 1024 * 1024,
            transcendentals=nb * NNB * BLK * BLK,
        ),
        name="attention",
    )(ids, counts, own, before, after)


def settle_kernel(main, grad_own, from_above, from_below, out):
    out[:, :2] = main[...]
    out[:, 2:] = (
        grad_own[...] + from_above[...].astype(F32) + from_below[...].astype(F32)
    ).astype(BF16)


def settle(main, grad_own, from_above, from_below):
    nb = main.shape[0]
    return pl.pallas_call(
        settle_kernel,
        out_shape=jax.ShapeDtypeStruct((nb, 4, BLK, HD), BF16),
        in_specs=[VMEM] * 4,
        out_specs=VMEM,
        compiler_params=pltpu.CompilerParams(vmem_limit_bytes=LIMIT),
        name="settle",
    )(main, grad_own, from_above, from_below)


def passed_along(value, axis, steps):
    count = lax.axis_size(axis)
    initial, last = (max(0, -steps), min(count, count - steps))
    return lax.ppermute(value, axis, [(source, source + steps) for source in range(initial, last)])


def exchange(value):
    return lax.all_to_all(value, "sp", split_axis=0, concat_axis=0, tiled=True)


def local(queries, key_rows, value_rows, upstream, neighbours, counts):
    sp = lax.axis_size("sp")
    heads_dev = H // sp
    nb = queries.shape[0] * sp // BLK
    ids = neighbours - (lax.axis_index("grp") - 1) * nb
    arrays = (key_rows, value_rows, queries, upstream)
    owned = [exchange(pack(arrays, phase, heads_dev, sp)) for phase in range(heads_dev)]
    outs = ()
    for phase, own in enumerate(owned):
        tables = own[:, :2]
        before = passed_along(tables, "grp", 1)
        after = passed_along(tables, "grp", -1)
        main, grad_own, grad_before, grad_after = attention(ids, counts, own, before, after)
        from_above = passed_along(grad_before, "grp", -1)
        from_below = passed_along(grad_after, "grp", 1)
        sent = exchange(settle(main, grad_own, from_above, from_below))
        outs = unpack(sent, outs, phase, heads_dev, sp)
    return tuple(outs)


def solution(mesh):
    rows = P(("grp", "sp"), None)
    return jax.shard_map(
        local,
        mesh=mesh,
        in_specs=(rows, rows, rows, rows, P("grp", None), P("grp")),
        out_specs=(rows, rows, rows, rows),
        check_vma=False,
    )
```

```python
import functools

import jax
import jax.numpy as jnp
from jax import lax
from jax.experimental import pallas as pl
from jax.experimental.pallas import tpu as pltpu
from jax.sharding import PartitionSpec as P

H = 16
HD = 128
BLK = 128
NNB = 8
PAIR = 8
SCALE = HD ** (-0.5)
LOG2E = 1.4426950408889634
NT = (((1,), (1,)), ((), ()))
NN = (((1,), (0,)), ((), ()))
TN = (((0,), (0,)), ((), ()))
F32 = jnp.float32
BF16 = jnp.bfloat16
ANY = pl.BlockSpec(memory_space=pltpu.HBM)
SMEM = pl.BlockSpec(memory_space=pltpu.SMEM)
VMEM = pl.BlockSpec(memory_space=pltpu.VMEM)
LIMIT = 28 * 1024 * 1024


def dot(a, b, dims):
    return lax.dot_general(a, b, dims, preferred_element_type=F32)


def run_copies(copies):
    for copy in copies:
        copy.start()
    for copy in copies:
        copy.wait()


def pack_kernel(spots, *refs):
    place, sources = refs[0], refs[1:3]
    outs, sems = refs[3:-1], refs[-1]
    n = len(outs)
    copies = []
    for d, out in enumerate(outs):
        owner = lax.rem(place[0] + d, n)
        for i, source in enumerate(sources):
            for h in range(spots):
                column = pl.multiple_of((owner * spots + h) * HD, HD)
                copies.append(
                    pltpu.make_async_copy(
                        source.at[:, pl.ds(column, HD)], out.at[h, i], sems.at[d, i, h]
                    )
                )
    run_copies(copies)


def pack(place, first, second, spots):
    rows, width = first.shape
    n = width // (spots * HD)
    return pl.pallas_call(
        functools.partial(pack_kernel, spots),
        out_shape=[jax.ShapeDtypeStruct((spots, 2, rows, HD), BF16)] * n,
        in_specs=[SMEM, ANY, ANY],
        out_specs=[VMEM] * n,
        scratch_shapes=[pltpu.SemaphoreType.DMA((n, 2, spots))],
        name="pack",
    )(place, first, second)


def unpack_kernel(spots, n, place, *refs):
    received, outs, sems = refs[:n], refs[n:n + 2], refs[-1]
    copies = []
    for r, value in enumerate(received):
        source = lax.rem(place[0] + r, n)
        for i, out in enumerate(outs):
            for h in range(spots):
                column = pl.multiple_of((source * spots + h) * HD, HD)
                copies.append(
                    pltpu.make_async_copy(
                        value.at[h, i], out.at[:, pl.ds(column, HD)], sems.at[r, i, h]
                    )
                )
    run_copies(copies)


def unpack(place, received):
    n = len(received)
    spots, _, rows, _ = received[0].shape
    return pl.pallas_call(
        functools.partial(unpack_kernel, spots, n),
        out_shape=[jax.ShapeDtypeStruct((rows, n * spots * HD), BF16)] * 2,
        in_specs=[SMEM] + [VMEM] * n,
        out_specs=[ANY] * 2,
        scratch_shapes=[pltpu.SemaphoreType.DMA((n, 2, spots))],
        name="unpack",
    )(place, *received)


def join_kernel(*refs):
    out, sems = refs[-2], refs[-1]
    run_copies(
        [pltpu.make_async_copy(x, out.at[r], sems.at[r]) for r, x in enumerate(refs[:-2])]
    )


def join(parts):
    n = len(parts)
    return pl.pallas_call(
        join_kernel,
        out_shape=jax.ShapeDtypeStruct((n, *parts[0].shape), BF16),
        in_specs=[ANY] * n,
        out_specs=VMEM,
        scratch_shapes=[pltpu.SemaphoreType.DMA((n,))],
        name="join",
    )(*parts)


def stack_kernel(spots, *refs):
    sources, out, sems = refs[:2], refs[2], refs[3]
    copies = []
    for j in range(out.shape[0]):
        for i, source in enumerate(sources):
            for h in range(spots):
                copies.append(
                    pltpu.make_async_copy(
                        source.at[:, pl.ds((j * spots + h) * HD, HD)],
                        out.at[j, h, i],
                        sems.at[j, i, h],
                    )
                )
    run_copies(copies)


def stack(first, second, spots):
    rows, width = first.shape
    n = width // (spots * HD)
    return pl.pallas_call(
        functools.partial(stack_kernel, spots),
        out_shape=jax.ShapeDtypeStruct((n, spots, 2, rows, HD), BF16),
        in_specs=[ANY] * 2,
        out_specs=VMEM,
        scratch_shapes=[pltpu.SemaphoreType.DMA((n, 2, spots))],
        name="stack",
    )(first, second)


def unstack_kernel(spots, value, first, second, sems):
    copies = []
    for j in range(value.shape[0]):
        for i, out in enumerate((first, second)):
            for h in range(spots):
                copies.append(
                    pltpu.make_async_copy(
                        value.at[j, h, i],
                        out.at[:, pl.ds((j * spots + h) * HD, HD)],
                        sems.at[j, i, h],
                    )
                )
    run_copies(copies)


def unstack(value):
    n, spots, _, rows, _ = value.shape
    return pl.pallas_call(
        functools.partial(unstack_kernel, spots),
        out_shape=[jax.ShapeDtypeStruct((rows, n * spots * HD), BF16)] * 2,
        in_specs=[VMEM],
        out_specs=[ANY] * 2,
        scratch_shapes=[pltpu.SemaphoreType.DMA((n, 2, spots))],
        name="unstack",
    )(value)


def join_kernel(*refs):
    out, sems = refs[-2], refs[-1]
    run_copies(
        [pltpu.make_async_copy(x, out.at[r], sems.at[r]) for r, x in enumerate(refs[:-2])]
    )


def join(parts):
    n = len(parts)
    return pl.pallas_call(
        join_kernel,
        out_shape=jax.ShapeDtypeStruct((n, *parts[0].shape), BF16),
        in_specs=[ANY] * n,
        out_specs=VMEM,
        scratch_shapes=[pltpu.SemaphoreType.DMA((n,))],
        name="join",
    )(*parts)


def attn_kernel(
    spots, nb, place, ids, counts, chip, own, link, rows,
    main_out, grad_chip, grad_own, grad_link, cache, acc, main, edge, soft, sems,
):
    here, offset, odd = place[0], place[1], place[2]
    chip_at = 2 * nb * (1 - odd)
    link_at = 2 * nb * odd
    copies = []
    for g, (x, at) in enumerate(((chip, chip_at), (own, nb), (link, link_at))):
        copies.append(pltpu.make_async_copy(x, cache.at[pl.ds(at, nb)], sems.at[g]))
    for copy in copies:
        copy.start()
    acc[...] = jnp.zeros_like(acc)
    for copy in copies:
        copy.wait()

    wide = PAIR * BLK

    def block(b, carry):
        used = counts[b]
        slots = []
        for j in range(NNB):
            local_id = ids[b, j] - offset
            side = local_id // nb
            slots.append(side * nb + lax.rem(here - (local_id - side * nb) + nb, nb))
        heads = range(spots)
        chunks = range(NNB // PAIR)
        lane_slot = lax.broadcasted_iota(jnp.int32, (1, wide), 1) // BLK

        def tile(h, i, c):
            return jnp.concatenate(
                [cache[s, h, i] for s in slots[c * PAIR:(c + 1) * PAIR]], axis=0
            )

        def span(c):
            return slice(c * wide, (c + 1) * wide)

        def add(h, i, c, part):
            for j, s in enumerate(slots[c * PAIR:(c + 1) * PAIR]):
                acc[s, h, i] += part[j * BLK:(j + 1) * BLK]

        queries = [rows[b, h, 0] for h in heads]
        grads = [rows[b, h, 1] for h in heads]
        highest, inverse, delta = [], [], []
        for h in heads:
            top = None
            for c in chunks:
                raw = dot(queries[h], tile(h, 0, c), NT)
                raw = jnp.where(lane_slot + c * PAIR < used, raw, -1e30)
                soft[h, :, span(c)] = raw
                top = raw if top is None else jnp.maximum(top, raw)
            highest.append(jnp.max(top, axis=1, keepdims=True))
        for h in heads:
            total = None
            for c in chunks:
                raised = jnp.exp2((soft[h, :, span(c)] - highest[h]) * (SCALE * LOG2E))
                soft[h, :, span(c)] = raised
                total = raised if total is None else total + raised
            inverse.append(1.0 / jnp.sum(total, axis=1, keepdims=True))
        for h in heads:
            out = None
            for c in chunks:
                weights = (soft[h, :, span(c)] * inverse[h]).astype(BF16)
                part = dot(weights, tile(h, 1, c), NN)
                out = part if out is None else out + part
                add(h, 1, c, dot(weights, grads[h], TN))
            attended = out.astype(BF16)
            main[b, h, 0] = attended
            delta.append(
                jnp.sum(grads[h].astype(F32) * attended.astype(F32), axis=1, keepdims=True)
            )
        for h in heads:
            out = None
            for c in chunks:
                grad_prob = dot(grads[h], tile(h, 1, c), NT)
                prob = soft[h, :, span(c)] * inverse[h]
                score = (prob * (grad_prob - delta[h])).astype(BF16)
                part = dot(score, tile(h, 0, c), NN)
                out = part if out is None else out + part
                add(h, 0, c, dot(score, queries[h], TN))
            main[b, h, 1] = (out * SCALE).astype(BF16)
        pltpu.make_async_copy(main.at[b], main_out.at[b], sems.at[3 + b]).start()
        return carry

    lax.fori_loop(0, nb, block, 0)
    copies = [
        pltpu.make_async_copy(main.at[b], main_out.at[b], sems.at[3 + b]) for b in range(nb)
    ]
    for i, (at, out) in enumerate(((link_at, grad_link), (chip_at, grad_chip))):
        part = pl.ds(at, nb)
        edge[i, :, :, 0] = (acc[part, :, 0] * SCALE).astype(BF16)
        edge[i, :, :, 1] = acc[part, :, 1].astype(BF16)
        copies.append(pltpu.make_async_copy(edge.at[i], out, sems.at[i]))
        copies[-1].start()
    copies.append(pltpu.make_async_copy(acc.at[pl.ds(nb, nb)], grad_own, sems.at[2]))
    copies[-1].start()
    for copy in copies:
        copy.wait()


def attention(place, ids, counts, rows, tables):
    shape = tables[0].shape
    nb, spots = shape[:2]
    whole = (3 * nb, *shape[1:])
    return pl.pallas_call(
        functools.partial(attn_kernel, spots, nb),
        out_shape=[jax.ShapeDtypeStruct(shape, kind) for kind in (BF16, BF16, F32, BF16)],
        in_specs=[SMEM] * 3 + [VMEM] * 4,
        out_specs=[ANY] * 4,
        scratch_shapes=[
            pltpu.VMEM(whole, BF16),
            pltpu.VMEM(whole, F32),
            pltpu.VMEM(shape, BF16),
            pltpu.VMEM((2, *shape), BF16),
            pltpu.VMEM((spots, BLK, NNB * BLK), F32),
            pltpu.SemaphoreType.DMA((3 + nb,)),
        ],
        compiler_params=pltpu.CompilerParams(vmem_limit_bytes=59 * 1024 * 1024),
        cost_estimate=pl.CostEstimate(
            flops=12 * spots * nb * NNB * BLK * BLK * HD,
            bytes_accessed=10 * 1024 * 1024,
            transcendentals=spots * nb * NNB * BLK * BLK,
        ),
        name="attention",
    )(place, ids, counts, *tables, rows)


def settle_kernel(grad_own, first, second, *outs):
    for r, out in enumerate(outs):
        for i, scale in enumerate((SCALE, 1.0)):
            total = grad_own[r, :, i] * scale
            total = total + first[r, :, i].astype(F32) + second[r, :, i].astype(F32)
            out[:, i] = total.astype(BF16)


def settle(grad_own, first, second):
    n = grad_own.shape[0]
    return pl.pallas_call(
        settle_kernel,
        out_shape=[jax.ShapeDtypeStruct(grad_own.shape[1:], BF16)] * n,
        in_specs=[VMEM] * 3,
        out_specs=[VMEM] * n,
        compiler_params=pltpu.CompilerParams(vmem_limit_bytes=LIMIT),
        name="settle",
    )(grad_own, first, second)


def swapped(value, start):
    pairs = [(i, i + 1) for i in range(start, lax.axis_size("grp") - 1, 2)]
    return lax.ppermute(value, "grp", pairs + [(j, i) for i, j in pairs])


def turned(value, steps):
    n = lax.axis_size("sp")
    if steps % n == 0:
        return value
    return lax.ppermute(value, "sp", [(i, (i + steps) % n) for i in range(n)])


def exchange(value):
    return lax.all_to_all(value, "sp", split_axis=0, concat_axis=0, tiled=True)


def follow(values, earlier):
    return lax.optimization_barrier((values, earlier))[0]


def local(queries, key_rows, value_rows, upstream, neighbours, counts):
    n = lax.axis_size("sp")
    spots = H // n
    nb = queries.shape[0] * n // BLK
    group = lax.axis_index("grp")
    place = jnp.stack([lax.axis_index("sp"), (group - 1) * nb, group % 2]).astype(jnp.int32)
    order = sorted(range(n), key=lambda d: -min(d, n - d))

    key_parts = pack(place, key_rows, value_rows, spots)
    row_parts = stack(*follow((queries, upstream), key_parts), spots)
    moved = [turned(key_parts[d], d) for d in order]
    moved, row_parts = lax.optimization_barrier((moved, row_parts))
    rows = exchange(row_parts)
    own = join([moved[order.index(d)] for d in range(n)])
    chip, link = swapped(own, 0), swapped(own, 1)
    main, grad_chip, grad_own, grad_link = attention(
        place, neighbours, counts, rows, (chip, own, link)
    )
    from_chip, from_link = swapped(grad_chip, 0), swapped(grad_link, 1)
    attended, query_grad = unstack(exchange(main))
    grads = settle(grad_own, from_chip, from_link)
    returned = [turned(grads[r], -r) for r in order]
    returned = follow(returned, (attended, query_grad))
    key_grad, value_grad = unpack(place, [returned[order.index(r)] for r in range(n)])
    return attended, query_grad, key_grad, value_grad


def solution(mesh):
    rows = P(("grp", "sp"), None)
    return jax.shard_map(
        local,
        mesh=mesh,
        in_specs=(rows, rows, rows, rows, P("grp", None), P("grp")),
        out_specs=(rows, rows, rows, rows),
        check_vma=False,
    )
```

```python
import functools

import jax
import jax.numpy as jnp
from jax import lax
from jax.experimental import pallas as pl
from jax.experimental.pallas import tpu as pltpu
from jax.sharding import PartitionSpec as P

H = 16
HD = 128
BLK = 128
NNB = 8
PAIR = 8
SCALE = HD ** (-0.5)
LOG2E = 1.4426950408889634
NT = (((1,), (1,)), ((), ()))
NN = (((1,), (0,)), ((), ()))
TN = (((0,), (0,)), ((), ()))
F32 = jnp.float32
BF16 = jnp.bfloat16
ANY = pl.BlockSpec(memory_space=pltpu.HBM)
SMEM = pl.BlockSpec(memory_space=pltpu.SMEM)
VMEM = pl.BlockSpec(memory_space=pltpu.VMEM)
LIMIT = 28 * 1024 * 1024


def dot(a, b, dims):
    return lax.dot_general(a, b, dims, preferred_element_type=F32)


def run_copies(copies):
    for copy in copies:
        copy.start()
    for copy in copies:
        copy.wait()


def pack_kernel(spots, *refs):
    sources, outs, sems = refs[:2], refs[2:-1], refs[-1]
    n = len(outs)
    here = lax.axis_index("sp")
    copies = []
    for d, out in enumerate(outs):
        owner = lax.rem(here + d, n)
        for i, source in enumerate(sources):
            for h in range(spots):
                column = pl.multiple_of((owner * spots + h) * HD, HD)
                copies.append(
                    pltpu.make_async_copy(
                        source.at[:, pl.ds(column, HD)], out.at[h, i], sems.at[d, i, h]
                    )
                )
    run_copies(copies)


def pack(first, second, spots):
    rows, width = first.shape
    n = width // (spots * HD)
    return pl.pallas_call(
        functools.partial(pack_kernel, spots),
        out_shape=[jax.ShapeDtypeStruct((spots, 2, rows, HD), BF16)] * n,
        in_specs=[ANY, ANY],
        out_specs=[VMEM] * n,
        scratch_shapes=[pltpu.SemaphoreType.DMA((n, 2, spots))],
        name="pack",
    )(first, second)


def unpack_kernel(spots, n, turns, *refs):
    received, outs, sems = refs[:len(turns)], refs[-3:-1], refs[-1]
    here = lax.axis_index("sp")
    copies = []
    for at, (turn, value) in enumerate(zip(turns, received)):
        source = lax.rem(here + turn, n)
        for i, out in enumerate(outs):
            for h in range(spots):
                column = pl.multiple_of((source * spots + h) * HD, HD)
                copies.append(
                    pltpu.make_async_copy(
                        value.at[h, i], out.at[:, pl.ds(column, HD)], sems.at[at, i, h]
                    )
                )
    run_copies(copies)


def unpack(turns, received, n, held=()):
    spots, _, rows, _ = received[0].shape
    count = len(turns)
    return pl.pallas_call(
        functools.partial(unpack_kernel, spots, n, turns),
        out_shape=[jax.ShapeDtypeStruct((rows, n * spots * HD), BF16)] * 2,
        in_specs=[VMEM] * count + [ANY] * len(held),
        out_specs=[ANY] * 2,
        input_output_aliases={count + i: i for i in range(len(held))},
        scratch_shapes=[pltpu.SemaphoreType.DMA((count, 2, spots))],
        name="unpack",
    )(*received, *held)


def join_kernel(*refs):
    out, sems = refs[-2], refs[-1]
    run_copies(
        [pltpu.make_async_copy(x, out.at[r], sems.at[r]) for r, x in enumerate(refs[:-2])]
    )


def join(parts):
    n = len(parts)
    return pl.pallas_call(
        join_kernel,
        out_shape=jax.ShapeDtypeStruct((n, *parts[0].shape), BF16),
        in_specs=[ANY] * n,
        out_specs=VMEM,
        scratch_shapes=[pltpu.SemaphoreType.DMA((n,))],
        name="join",
    )(*parts)


def stack_kernel(spots, *refs):
    sources, out, sems = refs[:2], refs[2], refs[3]
    copies = []
    for j in range(out.shape[0]):
        for i, source in enumerate(sources):
            for h in range(spots):
                copies.append(
                    pltpu.make_async_copy(
                        source.at[:, pl.ds((j * spots + h) * HD, HD)],
                        out.at[j, h, i],
                        sems.at[j, i, h],
                    )
                )
    run_copies(copies)


def stack(first, second, spots):
    rows, width = first.shape
    n = width // (spots * HD)
    return pl.pallas_call(
        functools.partial(stack_kernel, spots),
        out_shape=jax.ShapeDtypeStruct((n, spots, 2, rows, HD), BF16),
        in_specs=[ANY] * 2,
        out_specs=VMEM,
        scratch_shapes=[pltpu.SemaphoreType.DMA((n, 2, spots))],
        name="stack",
    )(first, second)


def unstack_kernel(spots, value, first, second, sems):
    copies = []
    for j in range(value.shape[0]):
        for i, out in enumerate((first, second)):
            for h in range(spots):
                copies.append(
                    pltpu.make_async_copy(
                        value.at[j, h, i],
                        out.at[:, pl.ds((j * spots + h) * HD, HD)],
                        sems.at[j, i, h],
                    )
                )
    run_copies(copies)


def unstack(value):
    n, spots, _, rows, _ = value.shape
    return pl.pallas_call(
        functools.partial(unstack_kernel, spots),
        out_shape=[jax.ShapeDtypeStruct((rows, n * spots * HD), BF16)] * 2,
        in_specs=[VMEM],
        out_specs=[ANY] * 2,
        scratch_shapes=[pltpu.SemaphoreType.DMA((n, 2, spots))],
        name="unstack",
    )(value)


def join_kernel(*refs):
    out, sems = refs[-2], refs[-1]
    run_copies(
        [pltpu.make_async_copy(x, out.at[r], sems.at[r]) for r, x in enumerate(refs[:-2])]
    )


def join(parts):
    n = len(parts)
    return pl.pallas_call(
        join_kernel,
        out_shape=jax.ShapeDtypeStruct((n, *parts[0].shape), BF16),
        in_specs=[ANY] * n,
        out_specs=VMEM,
        scratch_shapes=[pltpu.SemaphoreType.DMA((n,))],
        name="join",
    )(*parts)


def attn_kernel(
    spots, nb, ids, counts, chip, own, link, rows_in,
    main_out, grad_chip, grad_own, grad_link, rows, cache, acc, main, edge, sems,
):
    here, group = lax.axis_index("sp"), lax.axis_index("grp")
    offset, odd = (group - 1) * nb, lax.rem(group, 2)
    chip_at = 2 * nb * (1 - odd)
    link_at = 2 * nb * odd
    copies = [pltpu.make_async_copy(rows_in, rows, sems.at[3])]
    for g, (x, at) in enumerate(((chip, chip_at), (own, nb), (link, link_at))):
        copies.append(pltpu.make_async_copy(x, cache.at[pl.ds(at, nb)], sems.at[g]))
    for copy in copies:
        copy.start()
    acc[...] = jnp.zeros_like(acc)
    for copy in copies:
        copy.wait()

    def visit(b, used, width):
        slots = []
        for j in range(width):
            local_id = ids[b, j] - offset
            side = local_id // nb
            slots.append(side * nb + lax.rem(here - (local_id - side * nb) + nb, nb))
        heads = range(spots)
        lane_slot = lax.broadcasted_iota(jnp.int32, (1, width * BLK), 1) // BLK

        def tiles(h, i):
            return jnp.concatenate([cache[s, h, i] for s in slots], axis=0)

        queries = [rows[b, h, 0] for h in heads]
        grads = [rows[b, h, 1] for h in heads]
        probs = []
        for h in heads:
            raw = dot(queries[h], tiles(h, 0), NT)
            raw = jnp.where(lane_slot < used, raw, -1e30)
            highest = jnp.max(raw, axis=1, keepdims=True)
            raised = jnp.exp2((raw - highest) * (SCALE * LOG2E))
            probs.append(raised * (1.0 / jnp.sum(raised, axis=1, keepdims=True)))
        weights, deltas = [], []
        for h in heads:
            weights.append(probs[h].astype(BF16))
            attended = dot(weights[h], tiles(h, 1), NN).astype(BF16)
            main[b, h, 0] = attended
            deltas.append(
                jnp.sum(grads[h].astype(F32) * attended.astype(F32), axis=1, keepdims=True)
            )
        for h in heads:
            grad_prob = dot(grads[h], tiles(h, 1), NT)
            score = (probs[h] * (grad_prob - deltas[h])).astype(BF16)
            main[b, h, 1] = (dot(score, tiles(h, 0), NN) * SCALE).astype(BF16)
            key_part = dot(score, queries[h], TN)
            value_part = dot(weights[h], grads[h], TN)
            for j, s in enumerate(slots):
                acc[s, h, 0] += key_part[j * BLK:(j + 1) * BLK]
                acc[s, h, 1] += value_part[j * BLK:(j + 1) * BLK]
        pltpu.make_async_copy(main.at[b], main_out.at[b], sems.at[4 + b]).start()

    def block(b, carry):
        used = counts[b]
        for width in (2, 4, 6, 8):
            pl.when((used <= width) & (used > width - 2))(
                functools.partial(visit, b, used, width)
            )
        return carry

    lax.fori_loop(0, nb, block, 0)
    copies = [
        pltpu.make_async_copy(main.at[b], main_out.at[b], sems.at[4 + b]) for b in range(nb)
    ]
    copies.append(pltpu.make_async_copy(acc.at[pl.ds(nb, nb)], grad_own, sems.at[2]))
    copies[-1].start()
    for i, (at, out) in enumerate(((link_at, grad_link), (chip_at, grad_chip))):
        part = pl.ds(at, nb)
        edge[i, :, :, 0] = (acc[part, :, 0] * SCALE).astype(BF16)
        edge[i, :, :, 1] = acc[part, :, 1].astype(BF16)
        copies.append(pltpu.make_async_copy(edge.at[i], out, sems.at[i]))
        copies[-1].start()
    for copy in copies:
        copy.wait()


def attention(ids, counts, rows, tables):
    shape = tables[0].shape
    nb, spots = shape[:2]
    whole = (3 * nb, *shape[1:])
    sums = whole
    mine = shape
    return pl.pallas_call(
        functools.partial(attn_kernel, spots, nb),
        out_shape=[
            jax.ShapeDtypeStruct(shape, BF16),
            jax.ShapeDtypeStruct(shape, BF16),
            jax.ShapeDtypeStruct(mine, F32),
            jax.ShapeDtypeStruct(shape, BF16),
        ],
        in_specs=[SMEM] * 2 + [ANY] * 4,
        out_specs=[ANY] * 4,
        scratch_shapes=[
            pltpu.VMEM(shape, BF16),
            pltpu.VMEM(whole, BF16),
            pltpu.VMEM(sums, F32),
            pltpu.VMEM(shape, BF16),
            pltpu.VMEM((2, *shape), BF16),
            pltpu.SemaphoreType.DMA((4 + nb,)),
        ],
        compiler_params=pltpu.CompilerParams(vmem_limit_bytes=59 * 1024 * 1024),
        cost_estimate=pl.CostEstimate(
            flops=12 * spots * nb * NNB * BLK * BLK * HD,
            bytes_accessed=10 * 1024 * 1024,
            transcendentals=spots * nb * NNB * BLK * BLK,
        ),
        name="attention",
    )(ids, counts, *tables, rows)


def settle_kernel(grad_own, first, second, *outs):
    for r, out in enumerate(outs):
        for i, scale in enumerate((SCALE, 1.0)):
            total = grad_own[r, :, i] * scale
            total = total + first[r, :, i].astype(F32) + second[r, :, i].astype(F32)
            out[:, i] = total.astype(BF16)


def settle(grad_own, first, second):
    n = grad_own.shape[0]
    return pl.pallas_call(
        settle_kernel,
        out_shape=[jax.ShapeDtypeStruct(grad_own.shape[1:], BF16)] * n,
        in_specs=[VMEM] * 3,
        out_specs=[VMEM] * n,
        compiler_params=pltpu.CompilerParams(vmem_limit_bytes=LIMIT),
        name="settle",
    )(grad_own, first, second)


def swapped(value, start):
    pairs = [(i, i + 1) for i in range(start, lax.axis_size("grp") - 1, 2)]
    return lax.ppermute(value, "grp", pairs + [(j, i) for i, j in pairs])


def turned(value, steps):
    n = lax.axis_size("sp")
    if steps % n == 0:
        return value
    return lax.ppermute(value, "sp", [(i, (i + steps) % n) for i in range(n)])


def exchange(value):
    return lax.all_to_all(value, "sp", split_axis=0, concat_axis=0, tiled=True)


def follow(values, earlier):
    return lax.optimization_barrier((values, earlier))[0]


def local(queries, key_rows, value_rows, upstream, neighbours, counts):
    n = lax.axis_size("sp")
    spots = H // n
    nb = queries.shape[0] * n // BLK
    order = tuple(sorted(range(1, n), key=lambda d: -min(d, n - d)))

    key_parts = pack(key_rows, value_rows, spots)
    row_parts = stack(*follow((queries, upstream), key_parts), spots)
    moved = [turned(key_parts[d], d) for d in order]
    moved, row_parts = lax.optimization_barrier((moved, row_parts))
    rows = exchange(row_parts)
    own = join([key_parts[0], *(moved[order.index(d)] for d in range(1, n))])
    chip, link = swapped(own, 0), swapped(own, 1)
    main, grad_chip, grad_own, grad_link = attention(
        neighbours, counts, rows, (chip, own, link)
    )
    from_chip, from_link = swapped(grad_chip, 0), swapped(grad_link, 1)
    attended, query_grad = unstack(exchange(main))
    grads = settle(grad_own, from_chip, from_link)
    returned = [turned(grads[r], -r) for r in order]
    returned = follow(returned, (attended, query_grad))
    key_grad, value_grad = unpack((0, *order), [grads[0], *returned], n)
    return attended, query_grad, key_grad, value_grad


def solution(mesh):
    rows = P(("grp", "sp"), None)
    return jax.shard_map(
        local,
        mesh=mesh,
        in_specs=(rows, rows, rows, rows, P("grp", None), P("grp")),
        out_specs=(rows, rows, rows, rows),
        check_vma=False,
    )
```

```python
import functools

import jax
import jax.numpy as jnp
from jax import lax
from jax.experimental import pallas as pl
from jax.experimental.pallas import tpu as pltpu
from jax.sharding import PartitionSpec as P

H = 16
HD = 128
BLK = 128
NNB = 8
PAIR = 8
SCALE = HD ** (-0.5)
LOG2E = 1.4426950408889634
NT = (((1,), (1,)), ((), ()))
NN = (((1,), (0,)), ((), ()))
TN = (((0,), (0,)), ((), ()))
F32 = jnp.float32
BF16 = jnp.bfloat16
ANY = pl.BlockSpec(memory_space=pltpu.HBM)
SMEM = pl.BlockSpec(memory_space=pltpu.SMEM)
VMEM = pl.BlockSpec(memory_space=pltpu.VMEM)
LIMIT = 28 * 1024 * 1024


def dot(a, b, dims):
    return lax.dot_general(a, b, dims, preferred_element_type=F32)


def run_copies(copies):
    for copy in copies:
        copy.start()
    for copy in copies:
        copy.wait()


def pack_kernel(spots, n, first, second, *refs):
    outs, (staged, sems, sent) = refs[:n], refs[n:]
    here = lax.axis_index("sp")
    turns = sorted(range(n), key=lambda d: -min(d, n - d))
    copies = {}
    for d in turns:
        owner = lax.rem(here + d, n)
        copies[d] = []
        for i, source in enumerate((first, second)):
            for h in range(spots):
                column = pl.multiple_of((owner * spots + h) * HD, HD)
                copies[d].append(
                    pltpu.make_async_copy(
                        source.at[:, pl.ds(column, HD)], staged.at[d, h, i], sems.at[d, i, h]
                    )
                )
                copies[d][-1].start()
    leaving = []
    for d in turns:
        for copy in copies[d]:
            copy.wait()
        leaving.append(pltpu.make_async_copy(staged.at[d], outs[d], sent.at[d]))
        leaving[-1].start()
    for copy in leaving:
        copy.wait()


def pack(first, second, spots):
    rows, width = first.shape
    n = width // (spots * HD)
    return pl.pallas_call(
        functools.partial(pack_kernel, spots, n),
        out_shape=[jax.ShapeDtypeStruct((spots, 2, rows, HD), BF16)] * n,
        in_specs=[ANY, ANY],
        out_specs=[ANY] * n,
        scratch_shapes=[
            pltpu.VMEM((n, spots, 2, rows, HD), BF16),
            pltpu.SemaphoreType.DMA((n, 2, spots)),
            pltpu.SemaphoreType.DMA((n,)),
        ],
        name="pack",
    )(first, second)


def unpack_kernel(spots, n, turns, *refs):
    received, (first, second, staged, sems, sent) = refs[:len(turns)], refs[len(turns):]
    here = lax.axis_index("sp")
    arriving = []
    for at, value in enumerate(received):
        arriving.append(pltpu.make_async_copy(value, staged.at[at], sems.at[at]))
        arriving[-1].start()
    leaving = []
    for at, turn in enumerate(turns):
        source = lax.rem(here + turn, n)
        arriving[at].wait()
        for i, out in enumerate((first, second)):
            for h in range(spots):
                column = pl.multiple_of((source * spots + h) * HD, HD)
                leaving.append(
                    pltpu.make_async_copy(
                        staged.at[at, h, i], out.at[:, pl.ds(column, HD)], sent.at[at, i, h]
                    )
                )
                leaving[-1].start()
    for copy in leaving:
        copy.wait()


def unpack(turns, received, n):
    spots, _, rows, _ = received[0].shape
    count = len(turns)
    return pl.pallas_call(
        functools.partial(unpack_kernel, spots, n, turns),
        out_shape=[jax.ShapeDtypeStruct((rows, n * spots * HD), BF16)] * 2,
        in_specs=[ANY] * count,
        out_specs=[ANY] * 2,
        scratch_shapes=[
            pltpu.VMEM((count, spots, 2, rows, HD), BF16),
            pltpu.SemaphoreType.DMA((count,)),
            pltpu.SemaphoreType.DMA((count, 2, spots)),
        ],
        name="unpack",
    )(*received)


def join_kernel(*refs):
    out, sems = refs[-2], refs[-1]
    run_copies(
        [pltpu.make_async_copy(x, out.at[r], sems.at[r]) for r, x in enumerate(refs[:-2])]
    )


def join(parts):
    n = len(parts)
    return pl.pallas_call(
        join_kernel,
        out_shape=jax.ShapeDtypeStruct((n, *parts[0].shape), BF16),
        in_specs=[ANY] * n,
        out_specs=VMEM,
        scratch_shapes=[pltpu.SemaphoreType.DMA((n,))],
        name="join",
    )(*parts)


def stack_kernel(spots, *refs):
    sources, out, sems = refs[:2], refs[2], refs[3]
    copies = []
    for j in range(out.shape[0]):
        for i, source in enumerate(sources):
            for h in range(spots):
                copies.append(
                    pltpu.make_async_copy(
                        source.at[:, pl.ds((j * spots + h) * HD, HD)],
                        out.at[j, h, i],
                        sems.at[j, i, h],
                    )
                )
    run_copies(copies)


def stack(first, second, spots):
    rows, width = first.shape
    n = width // (spots * HD)
    return pl.pallas_call(
        functools.partial(stack_kernel, spots),
        out_shape=jax.ShapeDtypeStruct((n, spots, 2, rows, HD), BF16),
        in_specs=[ANY] * 2,
        out_specs=VMEM,
        scratch_shapes=[pltpu.SemaphoreType.DMA((n, 2, spots))],
        name="stack",
    )(first, second)


def unstack_kernel(spots, value, first, second, sems):
    copies = []
    for j in range(value.shape[0]):
        for i, out in enumerate((first, second)):
            for h in range(spots):
                copies.append(
                    pltpu.make_async_copy(
                        value.at[j, h, i],
                        out.at[:, pl.ds((j * spots + h) * HD, HD)],
                        sems.at[j, i, h],
                    )
                )
    run_copies(copies)


def unstack(value):
    n, spots, _, rows, _ = value.shape
    return pl.pallas_call(
        functools.partial(unstack_kernel, spots),
        out_shape=[jax.ShapeDtypeStruct((rows, n * spots * HD), BF16)] * 2,
        in_specs=[VMEM],
        out_specs=[ANY] * 2,
        scratch_shapes=[pltpu.SemaphoreType.DMA((n, 2, spots))],
        name="unstack",
    )(value)


def join_kernel(*refs):
    out, sems = refs[-2], refs[-1]
    run_copies(
        [pltpu.make_async_copy(x, out.at[r], sems.at[r]) for r, x in enumerate(refs[:-2])]
    )


def join(parts):
    n = len(parts)
    return pl.pallas_call(
        join_kernel,
        out_shape=jax.ShapeDtypeStruct((n, *parts[0].shape), BF16),
        in_specs=[ANY] * n,
        out_specs=VMEM,
        scratch_shapes=[pltpu.SemaphoreType.DMA((n,))],
        name="join",
    )(*parts)


def attn_kernel(
    spots, nb, ids, counts, chip, own, link, rows_in,
    main_out, grad_chip, grad_own, grad_link, rows, cache, acc, main, edge, sems,
):
    here, group = lax.axis_index("sp"), lax.axis_index("grp")
    offset, odd = (group - 1) * nb, lax.rem(group, 2)
    chip_at = 2 * nb * (1 - odd)
    link_at = 2 * nb * odd
    copies = [pltpu.make_async_copy(rows_in, rows, sems.at[3])]
    for g, (x, at) in enumerate(((chip, chip_at), (own, nb), (link, link_at))):
        copies.append(pltpu.make_async_copy(x, cache.at[pl.ds(at, nb)], sems.at[g]))
    for copy in copies:
        copy.start()
    acc[...] = jnp.zeros_like(acc)
    for copy in copies:
        copy.wait()

    def visit(b, used, width):
        slots = []
        for j in range(width):
            local_id = ids[b, j] - offset
            side = local_id // nb
            slots.append(side * nb + lax.rem(here - (local_id - side * nb) + nb, nb))
        heads = range(spots)
        lane_slot = lax.broadcasted_iota(jnp.int32, (1, width * BLK), 1) // BLK

        def tiles(h, i):
            return jnp.concatenate([cache[s, h, i] for s in slots], axis=0)

        queries = [rows[b, h, 0] for h in heads]
        grads = [rows[b, h, 1] for h in heads]
        probs = []
        for h in heads:
            raw = dot(queries[h], tiles(h, 0), NT)
            raw = jnp.where(lane_slot < used, raw, -1e30)
            highest = jnp.max(raw, axis=1, keepdims=True)
            raised = jnp.exp2((raw - highest) * (SCALE * LOG2E))
            probs.append(raised * (1.0 / jnp.sum(raised, axis=1, keepdims=True)))
        weights, deltas = [], []
        for h in heads:
            weights.append(probs[h].astype(BF16))
            attended = dot(weights[h], tiles(h, 1), NN).astype(BF16)
            main[b, h, 0] = attended
            deltas.append(
                jnp.sum(grads[h].astype(F32) * attended.astype(F32), axis=1, keepdims=True)
            )
        for h in heads:
            grad_prob = dot(grads[h], tiles(h, 1), NT)
            score = (probs[h] * (grad_prob - deltas[h])).astype(BF16)
            main[b, h, 1] = (dot(score, tiles(h, 0), NN) * SCALE).astype(BF16)
            key_part = dot(score, queries[h], TN)
            value_part = dot(weights[h], grads[h], TN)
            for j, s in enumerate(slots):
                acc[s, h, 0] += key_part[j * BLK:(j + 1) * BLK]
                acc[s, h, 1] += value_part[j * BLK:(j + 1) * BLK]
        pltpu.make_async_copy(main.at[b], main_out.at[b], sems.at[4 + b]).start()

    def block(b, carry):
        used = counts[b]
        for width in (2, 4, 6, 8):
            pl.when((used <= width) & (used > width - 2))(
                functools.partial(visit, b, used, width)
            )
        return carry

    lax.fori_loop(0, nb, block, 0)
    copies = [
        pltpu.make_async_copy(main.at[b], main_out.at[b], sems.at[4 + b]) for b in range(nb)
    ]
    copies.append(pltpu.make_async_copy(acc.at[pl.ds(nb, nb)], grad_own, sems.at[2]))
    copies[-1].start()
    for i, (at, out) in enumerate(((link_at, grad_link), (chip_at, grad_chip))):
        part = pl.ds(at, nb)
        edge[i, :, :, 0] = (acc[part, :, 0] * SCALE).astype(BF16)
        edge[i, :, :, 1] = acc[part, :, 1].astype(BF16)
        copies.append(pltpu.make_async_copy(edge.at[i], out, sems.at[i]))
        copies[-1].start()
    for copy in copies:
        copy.wait()


def attention(ids, counts, rows, tables):
    shape = tables[0].shape
    nb, spots = shape[:2]
    whole = (3 * nb, *shape[1:])
    sums = whole
    mine = shape
    return pl.pallas_call(
        functools.partial(attn_kernel, spots, nb),
        out_shape=[
            jax.ShapeDtypeStruct(shape, BF16),
            jax.ShapeDtypeStruct(shape, BF16),
            jax.ShapeDtypeStruct(mine, F32),
            jax.ShapeDtypeStruct(shape, BF16),
        ],
        in_specs=[SMEM] * 2 + [ANY] * 4,
        out_specs=[ANY] * 4,
        scratch_shapes=[
            pltpu.VMEM(shape, BF16),
            pltpu.VMEM(whole, BF16),
            pltpu.VMEM(sums, F32),
            pltpu.VMEM(shape, BF16),
            pltpu.VMEM((2, *shape), BF16),
            pltpu.SemaphoreType.DMA((4 + nb,)),
        ],
        compiler_params=pltpu.CompilerParams(vmem_limit_bytes=59 * 1024 * 1024),
        cost_estimate=pl.CostEstimate(
            flops=12 * spots * nb * NNB * BLK * BLK * HD,
            bytes_accessed=10 * 1024 * 1024,
            transcendentals=spots * nb * NNB * BLK * BLK,
        ),
        name="attention",
    )(ids, counts, *tables, rows)


def settle_kernel(grad_own, first, second, *outs):
    for r, out in enumerate(outs):
        for i, scale in enumerate((SCALE, 1.0)):
            total = grad_own[r, :, i] * scale
            total = total + first[r, :, i].astype(F32) + second[r, :, i].astype(F32)
            out[:, i] = total.astype(BF16)


def settle(grad_own, first, second):
    n = grad_own.shape[0]
    return pl.pallas_call(
        settle_kernel,
        out_shape=[jax.ShapeDtypeStruct(grad_own.shape[1:], BF16)] * n,
        in_specs=[VMEM] * 3,
        out_specs=[VMEM] * n,
        compiler_params=pltpu.CompilerParams(vmem_limit_bytes=LIMIT),
        name="settle",
    )(grad_own, first, second)


def swapped(value, start):
    pairs = [(i, i + 1) for i in range(start, lax.axis_size("grp") - 1, 2)]
    return lax.ppermute(value, "grp", pairs + [(j, i) for i, j in pairs])


def turned(value, steps):
    n = lax.axis_size("sp")
    if steps % n == 0:
        return value
    return lax.ppermute(value, "sp", [(i, (i + steps) % n) for i in range(n)])


def exchange(value):
    return lax.all_to_all(value, "sp", split_axis=0, concat_axis=0, tiled=True)


def follow(values, earlier):
    return lax.optimization_barrier((values, earlier))[0]


def local(queries, key_rows, value_rows, upstream, neighbours, counts):
    n = lax.axis_size("sp")
    spots = H // n
    nb = queries.shape[0] * n // BLK
    order = tuple(sorted(range(1, n), key=lambda d: -min(d, n - d)))

    key_parts = pack(key_rows, value_rows, spots)
    row_parts = stack(*follow((queries, upstream), key_parts), spots)
    moved = [turned(key_parts[d], d) for d in order]
    moved, row_parts = lax.optimization_barrier((moved, row_parts))
    rows = exchange(row_parts)
    own = join([key_parts[0], *(moved[order.index(d)] for d in range(1, n))])
    chip, link = swapped(own, 0), swapped(own, 1)
    main, grad_chip, grad_own, grad_link = attention(
        neighbours, counts, rows, (chip, own, link)
    )
    from_chip, from_link = swapped(grad_chip, 0), swapped(grad_link, 1)
    attended, query_grad = unstack(exchange(main))
    grads = settle(grad_own, from_chip, from_link)
    returned = [turned(grads[r], -r) for r in order]
    returned = follow(returned, (attended, query_grad))
    key_grad, value_grad = unpack((0, *order), [grads[0], *returned], n)
    return attended, query_grad, key_grad, value_grad


def solution(mesh):
    rows = P(("grp", "sp"), None)
    return jax.shard_map(
        local,
        mesh=mesh,
        in_specs=(rows, rows, rows, rows, P("grp", None), P("grp")),
        out_specs=(rows, rows, rows, rows),
        check_vma=False,
    )
```

```python
import functools

import jax
import jax.numpy as jnp
from jax import lax
from jax.experimental import pallas as pl
from jax.experimental.pallas import tpu as pltpu
from jax.sharding import PartitionSpec as P

H = 16
HD = 128
BLK = 128
NNB = 8
PAIR = 8
SCALE = HD ** (-0.5)
LOG2E = 1.4426950408889634
NT = (((1,), (1,)), ((), ()))
NN = (((1,), (0,)), ((), ()))
TN = (((0,), (0,)), ((), ()))
F32 = jnp.float32
BF16 = jnp.bfloat16
ANY = pl.BlockSpec(memory_space=pltpu.HBM)
SMEM = pl.BlockSpec(memory_space=pltpu.SMEM)
VMEM = pl.BlockSpec(memory_space=pltpu.VMEM)
LIMIT = 28 * 1024 * 1024


def dot(a, b, dims):
    return lax.dot_general(a, b, dims, preferred_element_type=F32)


def run_copies(copies):
    for copy in copies:
        copy.start()
    for copy in copies:
        copy.wait()


def pack_kernel(spots, n, first, second, *refs):
    outs, (staged, sems, sent) = refs[:n], refs[n:]
    here = lax.axis_index("sp")
    turns = sorted(range(n), key=lambda d: -min(d, n - d))
    copies = {}
    for d in turns:
        owner = lax.rem(here + d, n)
        copies[d] = []
        for i, source in enumerate((first, second)):
            for h in range(spots):
                column = pl.multiple_of((owner * spots + h) * HD, HD)
                copies[d].append(
                    pltpu.make_async_copy(
                        source.at[:, pl.ds(column, HD)], staged.at[d, h, i], sems.at[d, i, h]
                    )
                )
                copies[d][-1].start()
    leaving = []
    for d in turns:
        for copy in copies[d]:
            copy.wait()
        leaving.append(pltpu.make_async_copy(staged.at[d], outs[d], sent.at[d]))
        leaving[-1].start()
    for copy in leaving:
        copy.wait()


def pack(first, second, spots):
    rows, width = first.shape
    n = width // (spots * HD)
    return pl.pallas_call(
        functools.partial(pack_kernel, spots, n),
        out_shape=[jax.ShapeDtypeStruct((spots, 2, rows, HD), BF16)] * n,
        in_specs=[ANY, ANY],
        out_specs=[ANY] * n,
        scratch_shapes=[
            pltpu.VMEM((n, spots, 2, rows, HD), BF16),
            pltpu.SemaphoreType.DMA((n, 2, spots)),
            pltpu.SemaphoreType.DMA((n,)),
        ],
        name="pack",
    )(first, second)


def unpack_kernel(spots, n, turns, *refs):
    received, (first, second, staged, sems, sent) = refs[:len(turns)], refs[len(turns):]
    here = lax.axis_index("sp")
    arriving = []
    for at, value in enumerate(received):
        arriving.append(pltpu.make_async_copy(value, staged.at[at], sems.at[at]))
        arriving[-1].start()
    leaving = []
    for at, turn in enumerate(turns):
        source = lax.rem(here + turn, n)
        arriving[at].wait()
        for i, out in enumerate((first, second)):
            for h in range(spots):
                column = pl.multiple_of((source * spots + h) * HD, HD)
                leaving.append(
                    pltpu.make_async_copy(
                        staged.at[at, h, i], out.at[:, pl.ds(column, HD)], sent.at[at, i, h]
                    )
                )
                leaving[-1].start()
    for copy in leaving:
        copy.wait()


def unpack(turns, received, n):
    spots, _, rows, _ = received[0].shape
    count = len(turns)
    return pl.pallas_call(
        functools.partial(unpack_kernel, spots, n, turns),
        out_shape=[jax.ShapeDtypeStruct((rows, n * spots * HD), BF16)] * 2,
        in_specs=[ANY] * count,
        out_specs=[ANY] * 2,
        scratch_shapes=[
            pltpu.VMEM((count, spots, 2, rows, HD), BF16),
            pltpu.SemaphoreType.DMA((count,)),
            pltpu.SemaphoreType.DMA((count, 2, spots)),
        ],
        name="unpack",
    )(*received)


def join_kernel(*refs):
    out, sems = refs[-2], refs[-1]
    run_copies(
        [pltpu.make_async_copy(x, out.at[r], sems.at[r]) for r, x in enumerate(refs[:-2])]
    )


def join(parts):
    n = len(parts)
    return pl.pallas_call(
        join_kernel,
        out_shape=jax.ShapeDtypeStruct((n, *parts[0].shape), BF16),
        in_specs=[ANY] * n,
        out_specs=VMEM,
        scratch_shapes=[pltpu.SemaphoreType.DMA((n,))],
        name="join",
    )(*parts)


def stack_kernel(spots, *refs):
    sources, out, sems = refs[:2], refs[2], refs[3]
    copies = []
    for j in range(out.shape[0]):
        for i, source in enumerate(sources):
            for h in range(spots):
                copies.append(
                    pltpu.make_async_copy(
                        source.at[:, pl.ds((j * spots + h) * HD, HD)],
                        out.at[j, h, i],
                        sems.at[j, i, h],
                    )
                )
    run_copies(copies)


def stack(first, second, spots):
    rows, width = first.shape
    n = width // (spots * HD)
    return pl.pallas_call(
        functools.partial(stack_kernel, spots),
        out_shape=jax.ShapeDtypeStruct((n, spots, 2, rows, HD), BF16),
        in_specs=[ANY] * 2,
        out_specs=VMEM,
        scratch_shapes=[pltpu.SemaphoreType.DMA((n, 2, spots))],
        name="stack",
    )(first, second)


def unstack_kernel(spots, value, first, second, sems):
    copies = []
    for j in range(value.shape[0]):
        for i, out in enumerate((first, second)):
            for h in range(spots):
                copies.append(
                    pltpu.make_async_copy(
                        value.at[j, h, i],
                        out.at[:, pl.ds((j * spots + h) * HD, HD)],
                        sems.at[j, i, h],
                    )
                )
    run_copies(copies)


def unstack(value):
    n, spots, _, rows, _ = value.shape
    return pl.pallas_call(
        functools.partial(unstack_kernel, spots),
        out_shape=[jax.ShapeDtypeStruct((rows, n * spots * HD), BF16)] * 2,
        in_specs=[VMEM],
        out_specs=[ANY] * 2,
        scratch_shapes=[pltpu.SemaphoreType.DMA((n, 2, spots))],
        name="unstack",
    )(value)


def join_kernel(*refs):
    out, sems = refs[-2], refs[-1]
    run_copies(
        [pltpu.make_async_copy(x, out.at[r], sems.at[r]) for r, x in enumerate(refs[:-2])]
    )


def join(parts):
    n = len(parts)
    return pl.pallas_call(
        join_kernel,
        out_shape=jax.ShapeDtypeStruct((n, *parts[0].shape), BF16),
        in_specs=[ANY] * n,
        out_specs=VMEM,
        scratch_shapes=[pltpu.SemaphoreType.DMA((n,))],
        name="join",
    )(*parts)


def attn_kernel(
    spots, nb, ids, counts, chip, own, link, rows_in,
    main_out, grad_chip, grad_own, grad_link, rows, cache, acc, main, edge, sems,
):
    here, group = lax.axis_index("sp"), lax.axis_index("grp")
    offset, odd = (group - 1) * nb, lax.rem(group, 2)
    chip_at = 2 * nb * (1 - odd)
    link_at = 2 * nb * odd
    copies = [pltpu.make_async_copy(rows_in, rows, sems.at[3])]
    for g, (x, at) in enumerate(((chip, chip_at), (own, nb), (link, link_at))):
        copies.append(pltpu.make_async_copy(x, cache.at[pl.ds(at, nb)], sems.at[g]))
    for copy in copies:
        copy.start()
    acc[...] = jnp.zeros_like(acc)
    for copy in copies:
        copy.wait()

    def visit(b, used, width):
        slots = []
        for j in range(width):
            local_id = ids[b, j] - offset
            side = local_id // nb
            slots.append(side * nb + lax.rem(here - (local_id - side * nb) + nb, nb))
        heads = range(spots)

        def tiles(h, i):
            return jnp.concatenate([cache[s, h, i] for s in slots], axis=0)

        queries = [rows[b, h, 0] for h in heads]
        grads = [rows[b, h, 1] for h in heads]
        probs = []
        for h in heads:
            raw = dot(queries[h], tiles(h, 0), NT)
            final = jnp.where(used == width, raw[:, -BLK:], -1e30)
            raw = jnp.concatenate([raw[:, :-BLK], final], axis=1)
            highest = jnp.max(raw, axis=1, keepdims=True)
            raised = jnp.exp2((raw - highest) * (SCALE * LOG2E))
            probs.append(raised * (1.0 / jnp.sum(raised, axis=1, keepdims=True)))
        weights, deltas = [], []
        for h in heads:
            weights.append(probs[h].astype(BF16))
            attended = dot(weights[h], tiles(h, 1), NN).astype(BF16)
            main[b, h, 0] = attended
            deltas.append(
                jnp.sum(grads[h].astype(F32) * attended.astype(F32), axis=1, keepdims=True)
            )
        for h in heads:
            grad_prob = dot(grads[h], tiles(h, 1), NT)
            score = (probs[h] * (grad_prob - deltas[h])).astype(BF16)
            main[b, h, 1] = (dot(score, tiles(h, 0), NN) * SCALE).astype(BF16)
            key_part = dot(score, queries[h], TN)
            value_part = dot(weights[h], grads[h], TN)
            for j, s in enumerate(slots):
                acc[s, h, 0] += key_part[j * BLK:(j + 1) * BLK]
                acc[s, h, 1] += value_part[j * BLK:(j + 1) * BLK]
        pltpu.make_async_copy(main.at[b], main_out.at[b], sems.at[4 + b]).start()

    def block(b, carry):
        used = counts[b]
        for width in (2, 4, 6, 8):
            pl.when((used <= width) & (used > width - 2))(
                functools.partial(visit, b, used, width)
            )
        return carry

    lax.fori_loop(0, nb, block, 0)
    copies = [
        pltpu.make_async_copy(main.at[b], main_out.at[b], sems.at[4 + b]) for b in range(nb)
    ]
    copies.append(pltpu.make_async_copy(acc.at[pl.ds(nb, nb)], grad_own, sems.at[2]))
    copies[-1].start()
    for i, (at, out) in enumerate(((link_at, grad_link), (chip_at, grad_chip))):
        part = pl.ds(at, nb)
        edge[i, :, :, 0] = (acc[part, :, 0] * SCALE).astype(BF16)
        edge[i, :, :, 1] = acc[part, :, 1].astype(BF16)
        copies.append(pltpu.make_async_copy(edge.at[i], out, sems.at[i]))
        copies[-1].start()
    for copy in copies:
        copy.wait()


def attention(ids, counts, rows, tables):
    shape = tables[0].shape
    nb, spots = shape[:2]
    whole = (3 * nb, *shape[1:])
    sums = whole
    mine = shape
    return pl.pallas_call(
        functools.partial(attn_kernel, spots, nb),
        out_shape=[
            jax.ShapeDtypeStruct(shape, BF16),
            jax.ShapeDtypeStruct(shape, BF16),
            jax.ShapeDtypeStruct(mine, F32),
            jax.ShapeDtypeStruct(shape, BF16),
        ],
        in_specs=[SMEM] * 2 + [ANY] * 4,
        out_specs=[ANY] * 4,
        scratch_shapes=[
            pltpu.VMEM(shape, BF16),
            pltpu.VMEM(whole, BF16),
            pltpu.VMEM(sums, F32),
            pltpu.VMEM(shape, BF16),
            pltpu.VMEM((2, *shape), BF16),
            pltpu.SemaphoreType.DMA((4 + nb,)),
        ],
        compiler_params=pltpu.CompilerParams(vmem_limit_bytes=59 * 1024 * 1024),
        cost_estimate=pl.CostEstimate(
            flops=12 * spots * nb * NNB * BLK * BLK * HD,
            bytes_accessed=10 * 1024 * 1024,
            transcendentals=spots * nb * NNB * BLK * BLK,
        ),
        name="attention",
    )(ids, counts, *tables, rows)


def settle_kernel(grad_own, first, second, *outs):
    for r, out in enumerate(outs):
        for i, scale in enumerate((SCALE, 1.0)):
            total = grad_own[r, :, i] * scale
            total = total + first[r, :, i].astype(F32) + second[r, :, i].astype(F32)
            out[:, i] = total.astype(BF16)


def settle(grad_own, first, second):
    n = grad_own.shape[0]
    return pl.pallas_call(
        settle_kernel,
        out_shape=[jax.ShapeDtypeStruct(grad_own.shape[1:], BF16)] * n,
        in_specs=[VMEM] * 3,
        out_specs=[VMEM] * n,
        compiler_params=pltpu.CompilerParams(vmem_limit_bytes=LIMIT),
        name="settle",
    )(grad_own, first, second)


def swapped(value, start):
    pairs = [(i, i + 1) for i in range(start, lax.axis_size("grp") - 1, 2)]
    return lax.ppermute(value, "grp", pairs + [(j, i) for i, j in pairs])


def turned(value, steps):
    n = lax.axis_size("sp")
    if steps % n == 0:
        return value
    return lax.ppermute(value, "sp", [(i, (i + steps) % n) for i in range(n)])


def exchange(value):
    return lax.all_to_all(value, "sp", split_axis=0, concat_axis=0, tiled=True)


def follow(values, earlier):
    return lax.optimization_barrier((values, earlier))[0]


def local(queries, key_rows, value_rows, upstream, neighbours, counts):
    n = lax.axis_size("sp")
    spots = H // n
    nb = queries.shape[0] * n // BLK
    order = tuple(sorted(range(1, n), key=lambda d: -min(d, n - d)))

    key_parts = pack(key_rows, value_rows, spots)
    row_parts = stack(*follow((queries, upstream), key_parts), spots)
    moved = [turned(key_parts[d], d) for d in order]
    moved, row_parts = lax.optimization_barrier((moved, row_parts))
    rows = exchange(row_parts)
    own = join([key_parts[0], *(moved[order.index(d)] for d in range(1, n))])
    chip, link = swapped(own, 0), swapped(own, 1)
    main, grad_chip, grad_own, grad_link = attention(
        neighbours, counts, rows, (chip, own, link)
    )
    from_chip, from_link = swapped(grad_chip, 0), swapped(grad_link, 1)
    attended, query_grad = unstack(exchange(main))
    grads = settle(grad_own, from_chip, from_link)
    returned = [turned(grads[r], -r) for r in order]
    returned = follow(returned, (attended, query_grad))
    key_grad, value_grad = unpack((0, *order), [grads[0], *returned], n)
    return attended, query_grad, key_grad, value_grad


def solution(mesh):
    rows = P(("grp", "sp"), None)
    return jax.shard_map(
        local,
        mesh=mesh,
        in_specs=(rows, rows, rows, rows, P("grp", None), P("grp")),
        out_specs=(rows, rows, rows, rows),
        check_vma=False,
    )
```
